32 devices in a mesh: groups: 2 (over y), tensor: 4 (over z), sub: 4 (over x, core).
Axes of the slice: x: 2, y: 2, z: 4, core: 2. Of those that a mesh axis runs over, the one named last changes fastest.
Arguments:
- tokens: bfloat16 [256, 8192], P(('groups', 'tensor'), 'sub'), parts along dimension 0, may hold values from -6 to 6
- request_adapter_ids: int32 [2], P('groups'), parts along dimension 0, may hold values from 0 to 11
- slot_of_adapter: int32 [24], P('groups'), parts along dimension 0, may hold values from 0 to 11, each once
- gate_weight: bfloat16 [8192, 14336], P('sub', 'tensor'), may hold values from -0.0625 to 0.0625
- up_weight: bfloat16 [8192, 14336], P('sub', 'tensor'), may hold values from -0.0625 to 0.0625
- down_weight: bfloat16 [14336, 8192], P('tensor', 'sub'), may hold values from -0.046875 to 0.046875
- adapter_input_maps: bfloat16 [24, 8192, 128], P(('groups', 'tensor'), 'sub'), parts along dimension 0, may hold values from -0.0625 to 0.0625
- adapter_output_maps: bfloat16 [24, 2, 64, 14336], P(('groups', 'tensor'), None, 'sub'), parts along dimension 0, may hold values from -0.75 to 0.75
Outputs:
- layer_out: bfloat16 [256, 8192], P(('groups', 'tensor'), 'sub'), parts along dimension 0
The draws below stay inside these ranges and needn't reach their ends.
There are 2 independent parts, one for each index of `groups`. The reference program is written for one: setup_inputs(seed, part) draws one part's arguments, and reference() takes and returns one part's arrays. A program takes and returns all parts, laid end to end along the dimension named above; an argument that names none is the same for every part. Nothing has to cross between parts.
Inputs may be any that keep to these rules, and one draw needn't show every extreme that they name: `slot_of_adapter`: a permutation: every storage slot appears exactly once; slot k is stored at tensor index k // 3. `request_adapter_ids`: several requests may name the same adapter.
All inputs are finite; a program needn't handle non-finite values.
Results may differ from the reference program's by a relative error of at most 0.018.
Values may be sent and summed in bfloat16 or wider, within the bound.
A program may use at most 192 MiB of HBM per device.

```python
import jax
import jax.numpy as jnp
from jax import lax

MODEL_WIDTH = 8192
HIDDEN_UNITS = 14336
ADAPTER_RANK = 64
BLOCK = 128
TOKEN_ROWS = 128
REQ = 1
ADAPTER_COUNT = 12
N_TENSOR = 4
N_SUB = 4


def block_scale(own_key, extent, shards, least, high):
    level, own = 1.0, jax.random.fold_in(own_key, 6)
    for position, parts in shards:
        heights = jnp.exp(jax.random.uniform(jax.random.fold_in(own, position), (parts,), jnp.float32, least / len(shards), high / len(shards)))
        level = level * jnp.repeat(heights, extent[position] // parts).reshape([-1 if axis == position else 1 for axis in range(len(extent))])
    return level


def bell_draw(rng, shape, deviation, reach, cuts=(), kind=jnp.bfloat16):
    gain = block_scale(rng, shape, cuts, -0.22, 0.18) if cuts else 1.0
    entries = jax.random.normal(rng, shape, jnp.float32) * deviation * gain
    return jnp.minimum(jnp.maximum(entries, -reach), reach).astype(kind)


def setup_inputs(seed: int = 0, part: int = 0) -> dict:
    splits = jax.random.split(jax.random.key(seed), 9)
    part_keys = jax.random.split(jax.random.fold_in(splits[8], part), 9)
    tokens = bell_draw(part_keys[0], (TOKEN_ROWS, MODEL_WIDTH), 1.0, 6.0, ((0, 4), (1, 4)))
    request_adapter_ids = jax.random.randint(part_keys[1], (REQ,), 0, ADAPTER_COUNT).astype(jnp.int32)
    slot_of_adapter = jax.random.permutation(part_keys[2], ADAPTER_COUNT).astype(jnp.int32)
    gate_weight = bell_draw(splits[3], (MODEL_WIDTH, HIDDEN_UNITS), MODEL_WIDTH ** -0.5, 0.0625, ((0, 4), (1, 4)))
    up_weight = bell_draw(splits[4], (MODEL_WIDTH, HIDDEN_UNITS), MODEL_WIDTH ** -0.5, 0.0625, ((0, 4), (1, 4)))
    down_weight = bell_draw(splits[5], (HIDDEN_UNITS, MODEL_WIDTH), HIDDEN_UNITS ** -0.5, 0.046875, ((0, 4), (1, 4)))
    adapter_input_maps = bell_draw(part_keys[6], (ADAPTER_COUNT, MODEL_WIDTH, 2 * ADAPTER_RANK), MODEL_WIDTH ** -0.5, 0.0625, ((0, 4), (1, 4)))
    adapter_output_maps = bell_draw(part_keys[7], (ADAPTER_COUNT, 2, ADAPTER_RANK, HIDDEN_UNITS), ADAPTER_RANK ** -0.5, 0.75, ((0, 4), (2, 4)))
    return {"tokens": tokens, "request_adapter_ids": request_adapter_ids, "slot_of_adapter": slot_of_adapter, "gate_weight": gate_weight, "up_weight": up_weight, "down_weight": down_weight, "adapter_input_maps": adapter_input_maps, "adapter_output_maps": adapter_output_maps}


def reference(tokens, request_adapter_ids, slot_of_adapter, gate_weight, up_weight, down_weight, adapter_input_maps, adapter_output_maps):
    slot_numbers = jnp.take(slot_of_adapter, request_adapter_ids).astype(jnp.int32)
    request_rows = tokens.reshape(REQ, BLOCK, MODEL_WIDTH).astype(jnp.float32)
    down_weight_panel = jnp.take(adapter_input_maps, slot_numbers, axis=0).astype(jnp.float32)
    shrink = jnp.einsum("qcd,qdk->qck", request_rows, down_weight_panel).astype(jnp.bfloat16)
    shrink = shrink.reshape(REQ, BLOCK, 2, ADAPTER_RANK)
    up_weight_panel = jnp.take(adapter_output_maps, slot_numbers, axis=0)
    feat_block = MODEL_WIDTH // N_SUB
    rank_columns_block = ADAPTER_RANK // N_SUB
    gate_sum = jnp.zeros((TOKEN_ROWS, HIDDEN_UNITS), jnp.float32)
    up_sum = jnp.zeros((TOKEN_ROWS, HIDDEN_UNITS), jnp.float32)
    for sub_index in range(N_SUB):
        low_col = sub_index * feat_block
        tok_block = tokens[:, low_col:low_col + feat_block]
        gate_base_output = jnp.dot(tok_block, gate_weight[low_col:low_col + feat_block], preferred_element_type=jnp.float32)
        up_base_output = jnp.dot(tok_block, up_weight[low_col:low_col + feat_block], preferred_element_type=jnp.float32)
        rank_low = sub_index * rank_columns_block
        reduced_piece = shrink[:, :, :, rank_low:rank_low + rank_columns_block].astype(jnp.float32)
        panel_piece = up_weight_panel[:, :, rank_low:rank_low + rank_columns_block, :].astype(jnp.float32)
        adapter_correction = jnp.einsum("gtoz,gozy->gtoy", reduced_piece, panel_piece).reshape(TOKEN_ROWS, 2, HIDDEN_UNITS)
        gate_output_piece = lax.optimization_barrier((gate_base_output + adapter_correction[:, 0]).astype(jnp.bfloat16))
        up_output_piece = lax.optimization_barrier((up_base_output + adapter_correction[:, 1]).astype(jnp.bfloat16))
        gate_sum = gate_sum + gate_output_piece.astype(jnp.float32)
        up_sum = up_sum + up_output_piece.astype(jnp.float32)
    hidden = (jax.nn.silu(gate_sum) * up_sum).astype(jnp.bfloat16)
    hidden_block = HIDDEN_UNITS // N_TENSOR
    down_sum = jnp.zeros((TOKEN_ROWS, MODEL_WIDTH), jnp.float32)
    for tensor_index in range(N_TENSOR):
        low_unit = tensor_index * hidden_block
        down_part = jnp.dot(hidden[:, low_unit:low_unit + hidden_block], down_weight[low_unit:low_unit + hidden_block], preferred_element_type=jnp.float32)
        down_part = lax.optimization_barrier(down_part.astype(jnp.bfloat16))
        down_sum = down_sum + down_part.astype(jnp.float32)
    return (tokens.astype(jnp.float32) + down_sum).astype(jnp.bfloat16)
```

```python
import functools

import jax
import jax.numpy as jnp
from jax import lax
from jax.experimental import pallas as pl
from jax.experimental.pallas import tpu as pltpu
from jax.sharding import PartitionSpec as P

MESH = pl.DeviceIdType.MESH
F32 = jnp.float32
BF16 = jnp.bfloat16


def tile_of(width, choices):
    for choice in choices:
        if width % choice == 0:
            return choice
    return width


def aligned(index, size):
    return pl.ds(pl.multiple_of(index * size, size), size)


def block_kernel(
    cfg,
    ids_ref,
    slots_ref,
    tok_hbm,
    gate_hbm,
    up_hbm,
    down_hbm,
    imap_hbm,
    omap_hbm,
    out_ref,
    x_buf,
    w_buf,
    d_buf,
    imap,
    omap,
    b_send,
    b_recv,
    sh1_send,
    sh1_recv,
    sh2_send,
    sh2_recv,
    s_cols,
    acc,
    part,
    p_recv,
    x_send,
    x_recv,
    hid,
    d_part,
    d_recv,
    load_sem,
    w_sem,
    dw_sem,
    tok_s,
    tok_r,
    b_s,
    b_r,
    sh1_s,
    sh1_r,
    sh2_s,
    sh2_r,
    p_s,
    p_r,
    x_s,
    x_r,
    h_s,
    h_r,
    f_s,
    f_r,
    d_s,
    d_r,
):
    nt, ns, nreq, kept, rb, rank = cfg["nt"], cfg["ns"], cfg["req"], cfg["kept"], cfg["rb"], cfg["rank"]
    rows, hcols, dcols = cfg["rows"], cfg["hcols"], cfg["dcols"]
    tn, tw, dn, dw = cfg["tn"], cfg["tw"], cfg["dn"], cfg["dw"]
    nc, nd, lead = hcols // tn, dcols // dn, cfg["lead"]
    rpt, rps, blk, npair = rows // nt, rows // ns, rows // nreq, ns // 2
    rr = 2 * rb
    t = lax.axis_index("tensor")
    s = lax.axis_index("sub")
    pair, core = lax.div(s, 2), lax.rem(s, 2)
    mate = pair * 2 + (1 - core)
    t_peers = [lax.rem(t + i, nt) for i in range(1, nt)]
    s_peers = [lax.rem(s + i, ns) for i in range(1, ns)]
    j_peers = [lax.rem(pair + i, npair) for i in range(1, npair)]

    def remote(src, dst, ssem, rsem, dev):
        return pltpu.make_async_remote_copy(
            src_ref=src, dst_ref=dst, send_sem=ssem, recv_sem=rsem, device_id=dev, device_id_type=MESH
        )

    sent = []

    def send(*args):
        copy = remote(*args)
        copy.start()
        sent.append(copy)

    l_omap = pltpu.make_async_copy(omap_hbm, omap, load_sem.at[0])
    l_tok = pltpu.make_async_copy(tok_hbm, x_buf.at[aligned(t, rpt), :], load_sem.at[1])
    l_imap = pltpu.make_async_copy(imap_hbm, imap, load_sem.at[2])
    l_omap.start()
    l_tok.start()
    l_imap.start()
    l_w = []
    for k in range(nc):
        cols = pl.ds(k * tn, tn)
        pair_loads = [
            pltpu.make_async_copy(src.at[:, cols], w_buf.at[g, :, cols], w_sem.at[g, k])
            for g, src in enumerate((gate_hbm, up_hbm))
        ]
        for copy in pair_loads:
            copy.start()
        l_w.append(pair_loads)

    barrier = pltpu.get_barrier_semaphore()
    for p in t_peers:
        pl.semaphore_signal(barrier, inc=1, device_id={"tensor": p}, device_id_type=MESH)
    for p in s_peers:
        pl.semaphore_signal(barrier, inc=1, device_id={"sub": p}, device_id_type=MESH)
    pl.semaphore_wait(barrier, nt + ns - 2)

    for i, p in enumerate(t_peers):
        send(tok_hbm, x_buf.at[aligned(t, rpt), :], tok_s.at[i], tok_r.at[t], {"tensor": p})

    slots = [slots_ref[ids_ref[q]] for q in range(nreq)]
    local = [lax.rem(v, kept) for v in slots]
    mine = [jnp.where(lax.div(v, kept) == t, 1.0, 0.0).astype(F32) for v in slots]

    l_omap.wait()
    for q in range(nreq):
        for c in range(nt):
            theirs = omap[local[q], :, c * hcols : (c + 1) * hcols]
            b_send[c, q * rr : (q + 1) * rr, :] = (theirs.astype(F32) * mine[q]).astype(BF16)
    for k in range(nc):
        cols = pl.ds(k * tn, tn)
        for i, p in enumerate(t_peers):
            send(
                b_send.at[p, :, cols],
                b_recv.at[t, :, cols],
                b_s.at[i, k],
                b_r.at[t, k],
                {"tensor": p},
            )

    l_imap.wait()
    l_tok.wait()
    for p in t_peers:
        remote(tok_hbm, x_buf.at[aligned(p, rpt), :], tok_s.at[0], tok_r.at[p], {"tensor": p}).wait_recv()

    for q in range(nreq):
        span = slice(q * blk, (q + 1) * blk)
        piece = jnp.dot(x_buf[span, :], imap[local[q]], preferred_element_type=F32) * mine[q]
        flipped = piece.T
        for d in range(ns):
            sh1_send[d, 0:rb, span] = flipped[d * rb : (d + 1) * rb]
            sh1_send[d, rb:rr, span] = flipped[rank + d * rb : rank + (d + 1) * rb]
    for i, p in enumerate(s_peers):
        send(sh1_send.at[p], sh1_recv.at[s], sh1_s.at[i], sh1_r.at[s], {"sub": p})

    l_d = []
    for n in range(nd):
        cols = pl.ds(n * dn, dn)
        copy = pltpu.make_async_copy(down_hbm.at[:, cols], d_buf.at[:, cols], dw_sem.at[n])
        copy.start()
        l_d.append(copy)

    per = tn // tw

    def matmul(k):
        for copy in l_w[k]:
            copy.wait()

        def body(j, carry):
            g, c = lax.div(j, per), lax.rem(j, per)
            if per == 1:
                into, cols = pl.ds(0, tw), pl.ds(k * tn, tw)
            else:
                into, cols = aligned(c, tw), pl.ds(pl.multiple_of(k * tn + c * tw, 128), tw)
            acc[k % lead, g, :, into] = jnp.dot(x_buf[...], w_buf[g, :, cols], preferred_element_type=F32)
            return carry

        lax.fori_loop(0, 2 * per, body, 0)

    def finish(k):
        cols = pl.ds(k * tn, tn)
        for p in t_peers:
            remote(
                b_send.at[p, :, cols], b_recv.at[p, :, cols], b_s.at[0, k], b_r.at[p, k], {"tensor": p}
            ).wait_recv()
        total = b_send[t, :, cols].astype(F32)
        for p in t_peers:
            total += b_recv[p, :, cols].astype(F32)
        maps = total.astype(BF16)
        for g in range(2):
            for q in range(nreq):
                span = slice(q * blk, (q + 1) * blk)
                part[g, span, cols] = (
                    acc[k % lead, g, span, :]
                    + jnp.dot(s_cols[g, span, :], maps[q * rr : (q + 1) * rr], preferred_element_type=F32)
                ).astype(BF16)
        for j in j_peers + [pair]:
            send(
                part.at[:, aligned(2 * j + 1 - core, rps), cols],
                p_recv.at[j, :, :, cols],
                p_s.at[j, k],
                p_r.at[j, k],
                {"sub": mate},
            )

    def wait_mate(j, k):
        cols = pl.ds(k * tn, tn)
        remote(
            part.at[:, aligned(2 * j + 1 - core, rps), cols],
            p_recv.at[j, :, :, cols],
            p_s.at[j, k],
            p_r.at[j, k],
            {"sub": mate},
        ).wait_recv()

    def across(k):
        cols = pl.ds(k * tn, tn)
        for j in j_peers:
            wait_mate(j, k)
            x_send[j, :, :, cols] = (
                part[:, aligned(2 * j + core, rps), cols].astype(F32) + p_recv[j, :, :, cols].astype(F32)
            ).astype(BF16)
            send(
                x_send.at[j, :, :, cols],
                x_recv.at[pair, :, :, cols],
                x_s.at[j, k],
                x_r.at[pair, k],
                {"sub": 2 * j + core},
            )

    def activate(k):
        cols = pl.ds(k * tn, tn)
        wait_mate(pair, k)
        total = part[:, aligned(s, rps), cols].astype(F32) + p_recv[pair, :, :, cols].astype(F32)
        for j in j_peers:
            remote(
                x_send.at[j, :, :, cols],
                x_recv.at[j, :, :, cols],
                x_s.at[j, k],
                x_r.at[j, k],
                {"sub": 2 * j + core},
            ).wait_recv()
            total += x_recv[j, :, :, cols].astype(F32)
        gate, up = total[0], total[1]
        mine_rows = hid.at[aligned(s, rps), cols]
        hid[aligned(s, rps), cols] = (gate / (1.0 + jnp.exp(-gate)) * up).astype(BF16)
        for j in j_peers:
            send(mine_rows, mine_rows, h_s.at[j, k], h_r.at[pair, k], {"sub": 2 * j + core})
        send(mine_rows, mine_rows, f_s.at[pair, k], f_r.at[pair, k], {"sub": mate})

    def relay(k):
        cols = pl.ds(k * tn, tn)
        for j in j_peers:
            theirs = hid.at[aligned(2 * j + core, rps), cols]
            remote(theirs, theirs, h_s.at[j, k], h_r.at[j, k], {"sub": 2 * j + core}).wait_recv()
            send(theirs, theirs, f_s.at[j, k], f_r.at[j, k], {"sub": mate})

    matmul(0)

    mine_sum = sh1_send[s]
    for p in s_peers:
        remote(sh1_send.at[p], sh1_recv.at[p], sh1_s.at[0], sh1_r.at[p], {"sub": p}).wait_recv()
        mine_sum += sh1_recv[p]
    sh2_send[...] = mine_sum.astype(BF16)
    for i, p in enumerate(t_peers):
        send(sh2_send, sh2_recv.at[t], sh2_s.at[i], sh2_r.at[t], {"tensor": p})

    for k in range(1, lead):
        matmul(k)

    shrink = sh2_send[...].astype(F32)
    for p in t_peers:
        remote(sh2_send, sh2_recv.at[p], sh2_s.at[0], sh2_r.at[p], {"tensor": p}).wait_recv()
        shrink += sh2_recv[p].astype(F32)
    is_gate = lax.broadcasted_iota(jnp.int32, (rr, rows), 0) < rb
    for g, chosen in enumerate((jnp.where(is_gate, shrink, 0.0), jnp.where(is_gate, 0.0, shrink))):
        for q in range(nreq):
            span = slice(q * blk, (q + 1) * blk)
            s_cols[g, span, :] = chosen[:, span].T.astype(BF16)

    for k in range(nc + 3):
        if k < nc:
            finish(k)
            if k + lead < nc:
                matmul(k + lead)
        if 0 <= k - 1 < nc:
            across(k - 1)
        if 0 <= k - 2 < nc:
            activate(k - 2)
        if 0 <= k - 3 < nc:
            relay(k - 3)

    for k in range(nc):
        cols = pl.ds(k * tn, tn)
        for j in j_peers + [pair]:
            theirs = hid.at[aligned(2 * j + 1 - core, rps), cols]
            remote(theirs, theirs, f_s.at[j, k], f_r.at[j, k], {"sub": mate}).wait_recv()

    for n in range(nd):
        l_d[n].wait()

        def down(c, carry, n=n):
            cols = pl.ds(pl.multiple_of(n * dn + c * dw, 128), dw)
            d_part[:, cols] = jnp.dot(hid[...], d_buf[:, cols], preferred_element_type=F32).astype(BF16)
            return carry

        lax.fori_loop(0, dn // dw, down, 0)
        cols = pl.ds(n * dn, dn)
        for i, p in enumerate(t_peers):
            send(
                d_part.at[aligned(p, rpt), cols],
                d_recv.at[t, :, cols],
                d_s.at[i, n],
                d_r.at[t, n],
                {"tensor": p},
            )

    for n in range(nd):
        cols = pl.ds(n * dn, dn)
        total = d_part[aligned(t, rpt), cols].astype(F32)
        for p in t_peers:
            remote(
                d_part.at[aligned(p, rpt), cols],
                d_recv.at[p, :, cols],
                d_s.at[0, n],
                d_r.at[p, n],
                {"tensor": p},
            ).wait_recv()
            total += d_recv[p, :, cols].astype(F32)
        out_ref[:, cols] = (x_buf[aligned(t, rpt), cols].astype(F32) + total).astype(BF16)

    for copy in sent:
        copy.wait_send()


def shards(mesh, tokens, ids, slots, gate_w, up_w, down_w, imaps, omaps):
    nt, ns = mesh.shape["tensor"], mesh.shape["sub"]
    kept, fcols, rank2 = imaps.shape
    rb = omaps.shape[2]
    rr = 2 * rb
    nreq = ids.shape[0]
    rpt = tokens.shape[0]
    rows = rpt * nt
    hcols, dcols = gate_w.shape[1], down_w.shape[1]
    rps, npair = rows // ns, ns // 2
    tn = tile_of(hcols, (512, 896, 384, 256, 128))
    tw = tile_of(tn, (256, 128))
    dn = tile_of(dcols, (512, 256, 128))
    dw = tile_of(dn, (256, 128))
    nc, nd = hcols // tn, dcols // dn
    lead = min(2, nc)
    cfg = dict(
        nt=nt, ns=ns, req=nreq, kept=kept, rb=rb, rank=rank2 // 2, rows=rows, hcols=hcols, dcols=dcols,
        tn=tn, tw=tw, dn=dn, dw=dw, lead=lead,
    )
    omaps = omaps.reshape(kept, rr, omaps.shape[3])
    dma = pltpu.SemaphoreType.DMA
    scratch = [
        pltpu.VMEM((rows, fcols), BF16),
        pltpu.VMEM((2, fcols, hcols), BF16),
        pltpu.VMEM((hcols, dcols), BF16),
        pltpu.VMEM(imaps.shape, BF16),
        pltpu.VMEM(omaps.shape, BF16),
        pltpu.VMEM((nt, nreq * rr, hcols), BF16),
        pltpu.VMEM((nt, nreq * rr, hcols), BF16),
        pltpu.VMEM((ns, rr, rows), F32),
        pltpu.VMEM((ns, rr, rows), F32),
        pltpu.VMEM((rr, rows), BF16),
        pltpu.VMEM((nt, rr, rows), BF16),
        pltpu.VMEM((2, rows, rr), BF16),
        pltpu.VMEM((lead, 2, rows, tn), F32),
        pltpu.VMEM((2, rows, hcols), BF16),
        pltpu.VMEM((npair, 2, rps, hcols), BF16),
        pltpu.VMEM((npair, 2, rps, hcols), BF16),
        pltpu.VMEM((npair, 2, rps, hcols), BF16),
        pltpu.VMEM((rows, hcols), BF16),
        pltpu.VMEM((rows, dcols), BF16),
        pltpu.VMEM((nt, rpt, dcols), BF16),
        dma((3,)),
        dma((2, nc)),
        dma((nd,)),
        dma((nt,)), dma((nt,)),
        dma((nt, nc)), dma((nt, nc)),
        dma((ns,)), dma((ns,)),
        dma((nt,)), dma((nt,)),
        dma((npair, nc)), dma((npair, nc)),
        dma((npair, nc)), dma((npair, nc)),
        dma((npair, nc)), dma((npair, nc)),
        dma((npair, nc)), dma((npair, nc)),
        dma((nt, nd)), dma((nt, nd)),
    ]
    any_space = pl.BlockSpec(memory_space=pl.ANY)
    smem = pl.BlockSpec(memory_space=pltpu.SMEM)
    weight_bytes = 2 * (2 * fcols * hcols + hcols * dcols)
    return pl.pallas_call(
        functools.partial(block_kernel, cfg),
        out_shape=jax.ShapeDtypeStruct((rpt, dcols), BF16),
        in_specs=[smem, smem] + [any_space] * 6,
        out_specs=pl.BlockSpec(memory_space=pltpu.VMEM),
        scratch_shapes=scratch,
        compiler_params=pltpu.CompilerParams(
            collective_id=0, has_side_effects=True, vmem_limit_bytes=60 * 1024 * 1024
        ),
        cost_estimate=pl.CostEstimate(
            flops=rows * weight_bytes, bytes_accessed=weight_bytes, transcendentals=rps * hcols
        ),
    )(ids, slots, tokens, gate_w, up_w, down_w, imaps, omaps)


def solution(mesh):
    in_specs = (
        P(("groups", "tensor"), "sub"),
        P("groups"),
        P("groups"),
        P("sub", "tensor"),
        P("sub", "tensor"),
        P("tensor", "sub"),
        P(("groups", "tensor"), "sub", None),
        P(("groups", "tensor"), None, "sub", None),
    )
    out_specs = P(("groups", "tensor"), "sub")
    return jax.shard_map(
        functools.partial(shards, mesh), mesh=mesh, in_specs=in_specs, out_specs=out_specs, check_vma=False
    )
```

```python
import functools

import jax
import jax.numpy as jnp
from jax import lax
from jax.experimental import pallas as pl
from jax.experimental.pallas import tpu as pltpu
from jax.sharding import PartitionSpec as P

MESH = pl.DeviceIdType.MESH
F32 = jnp.float32
BF16 = jnp.bfloat16


def tile_of(width, choices):
    for choice in choices:
        if width % choice == 0:
            return choice
    return width


def aligned(index, size):
    return pl.ds(pl.multiple_of(index * size, size), size)


def block_kernel(
    cfg,
    ids_ref,
    slots_ref,
    tok_hbm,
    gate_hbm,
    up_hbm,
    down_hbm,
    imap_hbm,
    omap_hbm,
    out_ref,
    x_buf,
    w_buf,
    d_buf,
    imap,
    omap,
    b_send,
    b_recv,
    sh1_send,
    sh1_recv,
    sh2_send,
    sh2_recv,
    s_cols,
    acc,
    part,
    p_recv,
    x_send,
    x_recv,
    hid,
    d_part,
    d_recv,
    load_sem,
    w_sem,
    dw_sem,
    tok_s,
    tok_r,
    b_s,
    b_r,
    sh1_s,
    sh1_r,
    sh2_s,
    sh2_r,
    p_s,
    p_r,
    x_s,
    x_r,
    h_s,
    h_r,
    f_s,
    f_r,
    d_s,
    d_r,
):
    nt, ns, nreq, kept, rb, rank = cfg["nt"], cfg["ns"], cfg["req"], cfg["kept"], cfg["rb"], cfg["rank"]
    rows, hcols, dcols = cfg["rows"], cfg["hcols"], cfg["dcols"]
    tn, tw, dn, dw = cfg["tn"], cfg["tw"], cfg["dn"], cfg["dw"]
    nc, nd, lead = hcols // tn, dcols // dn, cfg["lead"]
    rpt, rps, blk, npair = rows // nt, rows // ns, rows // nreq, ns // 2
    rr = 2 * rb
    t = lax.axis_index("tensor")
    s = lax.axis_index("sub")
    pair, core = lax.div(s, 2), lax.rem(s, 2)
    mate = pair * 2 + (1 - core)
    t_peers = [lax.rem(t + i, nt) for i in range(1, nt)]
    s_peers = [lax.rem(s + i, ns) for i in range(1, ns)]
    j_peers = [lax.rem(pair + i, npair) for i in range(1, npair)]

    def remote(src, dst, ssem, rsem, dev):
        return pltpu.make_async_remote_copy(
            src_ref=src, dst_ref=dst, send_sem=ssem, recv_sem=rsem, device_id=dev, device_id_type=MESH
        )

    sent = []

    def send(*args):
        copy = remote(*args)
        copy.start()
        sent.append(copy)

    l_omap = pltpu.make_async_copy(omap_hbm, omap, load_sem.at[0])
    l_tok = pltpu.make_async_copy(tok_hbm, x_buf.at[aligned(t, rpt), :], load_sem.at[1])
    l_imap = pltpu.make_async_copy(imap_hbm, imap, load_sem.at[2])
    l_omap.start()
    l_tok.start()
    l_imap.start()
    l_w = []
    for k in range(nc):
        cols = pl.ds(k * tn, tn)
        pair_loads = [
            pltpu.make_async_copy(src.at[:, cols], w_buf.at[g, :, cols], w_sem.at[g, k])
            for g, src in enumerate((gate_hbm, up_hbm))
        ]
        for copy in pair_loads:
            copy.start()
        l_w.append(pair_loads)

    barrier = pltpu.get_barrier_semaphore()
    for p in t_peers:
        pl.semaphore_signal(barrier, inc=1, device_id={"tensor": p}, device_id_type=MESH)
    for p in s_peers:
        pl.semaphore_signal(barrier, inc=1, device_id={"sub": p}, device_id_type=MESH)
    pl.semaphore_wait(barrier, nt + ns - 2)

    for i, p in enumerate(t_peers):
        send(tok_hbm, x_buf.at[aligned(t, rpt), :], tok_s.at[i], tok_r.at[t], {"tensor": p})

    slots = [slots_ref[ids_ref[q]] for q in range(nreq)]
    local = [lax.rem(v, kept) for v in slots]
    mine = [jnp.where(lax.div(v, kept) == t, 1.0, 0.0).astype(F32) for v in slots]

    l_omap.wait()
    for q in range(nreq):
        for c in range(nt):
            theirs = omap[local[q], :, c * hcols : (c + 1) * hcols]
            b_send[c, q * rr : (q + 1) * rr, :] = (theirs.astype(F32) * mine[q]).astype(BF16)
    map_copies = []

    def send_maps():
        k = len(map_copies)
        if k == nc:
            return
        if k > 0:
            for copy in map_copies[-1]:
                copy.wait_send()
        cols = pl.ds(k * tn, tn)
        copies = [
            remote(b_send.at[p, :, cols], b_recv.at[t, :, cols], b_s.at[i, k], b_r.at[t, k], {"tensor": p})
            for i, p in enumerate(t_peers)
        ]
        for copy in copies:
            copy.start()
        map_copies.append(copies)

    send_maps()
    l_imap.wait()
    l_tok.wait()
    for p in t_peers:
        remote(tok_hbm, x_buf.at[aligned(p, rpt), :], tok_s.at[0], tok_r.at[p], {"tensor": p}).wait_recv()

    for q in range(nreq):
        span = slice(q * blk, (q + 1) * blk)
        piece = jnp.dot(x_buf[span, :], imap[local[q]], preferred_element_type=F32) * mine[q]
        flipped = piece.T
        for d in range(ns):
            sh1_send[d, 0:rb, span] = flipped[d * rb : (d + 1) * rb]
            sh1_send[d, rb:rr, span] = flipped[rank + d * rb : rank + (d + 1) * rb]
    for i, p in enumerate(s_peers):
        send(sh1_send.at[p], sh1_recv.at[s], sh1_s.at[i], sh1_r.at[s], {"sub": p})

    send_maps()
    l_d = []
    for n in range(nd):
        cols = pl.ds(n * dn, dn)
        copy = pltpu.make_async_copy(down_hbm.at[:, cols], d_buf.at[:, cols], dw_sem.at[n])
        copy.start()
        l_d.append(copy)

    per = tn // tw

    def matmul(k):
        for copy in l_w[k]:
            copy.wait()

        def body(j, carry):
            g, c = lax.div(j, per), lax.rem(j, per)
            if per == 1:
                into, cols = pl.ds(0, tw), pl.ds(k * tn, tw)
            else:
                into, cols = aligned(c, tw), pl.ds(pl.multiple_of(k * tn + c * tw, 128), tw)
            acc[k % lead, g, :, into] = jnp.dot(x_buf[...], w_buf[g, :, cols], preferred_element_type=F32)
            return carry

        lax.fori_loop(0, 2 * per, body, 0)

    def finish(k):
        send_maps()
        cols = pl.ds(k * tn, tn)
        for p in t_peers:
            remote(
                b_send.at[p, :, cols], b_recv.at[p, :, cols], b_s.at[0, k], b_r.at[p, k], {"tensor": p}
            ).wait_recv()
        total = b_send[t, :, cols].astype(F32)
        for p in t_peers:
            total += b_recv[p, :, cols].astype(F32)
        maps = total.astype(BF16)
        for g in range(2):
            for q in range(nreq):
                span = slice(q * blk, (q + 1) * blk)
                part[g, span, cols] = (
                    acc[k % lead, g, span, :]
                    + jnp.dot(s_cols[g, span, :], maps[q * rr : (q + 1) * rr], preferred_element_type=F32)
                ).astype(BF16)
        for j in j_peers + [pair]:
            send(
                part.at[:, aligned(2 * j + 1 - core, rps), cols],
                p_recv.at[j, :, :, cols],
                p_s.at[j, k],
                p_r.at[j, k],
                {"sub": mate},
            )

    def wait_mate(j, k):
        cols = pl.ds(k * tn, tn)
        remote(
            part.at[:, aligned(2 * j + 1 - core, rps), cols],
            p_recv.at[j, :, :, cols],
            p_s.at[j, k],
            p_r.at[j, k],
            {"sub": mate},
        ).wait_recv()

    def across(k):
        cols = pl.ds(k * tn, tn)
        for j in j_peers:
            wait_mate(j, k)
            x_send[j, :, :, cols] = (
                part[:, aligned(2 * j + core, rps), cols].astype(F32) + p_recv[j, :, :, cols].astype(F32)
            ).astype(BF16)
            send(
                x_send.at[j, :, :, cols],
                x_recv.at[pair, :, :, cols],
                x_s.at[j, k],
                x_r.at[pair, k],
                {"sub": 2 * j + core},
            )

    def activate(k):
        cols = pl.ds(k * tn, tn)
        wait_mate(pair, k)
        total = part[:, aligned(s, rps), cols].astype(F32) + p_recv[pair, :, :, cols].astype(F32)
        for j in j_peers:
            remote(
                x_send.at[j, :, :, cols],
                x_recv.at[j, :, :, cols],
                x_s.at[j, k],
                x_r.at[j, k],
                {"sub": 2 * j + core},
            ).wait_recv()
            total += x_recv[j, :, :, cols].astype(F32)
        gate, up = total[0], total[1]
        mine_rows = hid.at[aligned(s, rps), cols]
        hid[aligned(s, rps), cols] = (gate / (1.0 + jnp.exp(-gate)) * up).astype(BF16)
        for j in j_peers:
            send(mine_rows, mine_rows, h_s.at[j, k], h_r.at[pair, k], {"sub": 2 * j + core})
        send(mine_rows, mine_rows, f_s.at[pair, k], f_r.at[pair, k], {"sub": mate})

    def relay(k):
        cols = pl.ds(k * tn, tn)
        for j in j_peers:
            theirs = hid.at[aligned(2 * j + core, rps), cols]
            remote(theirs, theirs, h_s.at[j, k], h_r.at[j, k], {"sub": 2 * j + core}).wait_recv()
            send(theirs, theirs, f_s.at[j, k], f_r.at[j, k], {"sub": mate})

    matmul(0)

    mine_sum = sh1_send[s]
    for p in s_peers:
        remote(sh1_send.at[p], sh1_recv.at[p], sh1_s.at[0], sh1_r.at[p], {"sub": p}).wait_recv()
        mine_sum += sh1_recv[p]
    sh2_send[...] = mine_sum.astype(BF16)
    for i, p in enumerate(t_peers):
        send(sh2_send, sh2_recv.at[t], sh2_s.at[i], sh2_r.at[t], {"tensor": p})

    send_maps()
    for k in range(1, lead):
        matmul(k)

    shrink = sh2_send[...].astype(F32)
    for p in t_peers:
        remote(sh2_send, sh2_recv.at[p], sh2_s.at[0], sh2_r.at[p], {"tensor": p}).wait_recv()
        shrink += sh2_recv[p].astype(F32)
    is_gate = lax.broadcasted_iota(jnp.int32, (rr, rows), 0) < rb
    for g, chosen in enumerate((jnp.where(is_gate, shrink, 0.0), jnp.where(is_gate, 0.0, shrink))):
        for q in range(nreq):
            span = slice(q * blk, (q + 1) * blk)
            s_cols[g, span, :] = chosen[:, span].T.astype(BF16)

    for k in range(nc + 3):
        if k < nc:
            finish(k)
            if k + lead < nc:
                matmul(k + lead)
        if 0 <= k - 1 < nc:
            across(k - 1)
        if 0 <= k - 2 < nc:
            activate(k - 2)
        if 0 <= k - 3 < nc:
            relay(k - 3)

    for k in range(nc):
        cols = pl.ds(k * tn, tn)
        for j in j_peers + [pair]:
            theirs = hid.at[aligned(2 * j + 1 - core, rps), cols]
            remote(theirs, theirs, f_s.at[j, k], f_r.at[j, k], {"sub": mate}).wait_recv()

    for n in range(nd):
        l_d[n].wait()

        def down(c, carry, n=n):
            cols = pl.ds(pl.multiple_of(n * dn + c * dw, 128), dw)
            d_part[:, cols] = jnp.dot(hid[...], d_buf[:, cols], preferred_element_type=F32).astype(BF16)
            return carry

        lax.fori_loop(0, dn // dw, down, 0)
        cols = pl.ds(n * dn, dn)
        for i, p in enumerate(t_peers):
            send(
                d_part.at[aligned(p, rpt), cols],
                d_recv.at[t, :, cols],
                d_s.at[i, n],
                d_r.at[t, n],
                {"tensor": p},
            )

    for n in range(nd):
        cols = pl.ds(n * dn, dn)
        total = d_part[aligned(t, rpt), cols].astype(F32)
        for p in t_peers:
            remote(
                d_part.at[aligned(p, rpt), cols],
                d_recv.at[p, :, cols],
                d_s.at[0, n],
                d_r.at[p, n],
                {"tensor": p},
            ).wait_recv()
            total += d_recv[p, :, cols].astype(F32)
        out_ref[:, cols] = (x_buf[aligned(t, rpt), cols].astype(F32) + total).astype(BF16)

    for copy in map_copies[-1] + sent:
        copy.wait_send()


def shards(mesh, tokens, ids, slots, gate_w, up_w, down_w, imaps, omaps):
    nt, ns = mesh.shape["tensor"], mesh.shape["sub"]
    kept, fcols, rank2 = imaps.shape
    rb = omaps.shape[2]
    rr = 2 * rb
    nreq = ids.shape[0]
    rpt = tokens.shape[0]
    rows = rpt * nt
    hcols, dcols = gate_w.shape[1], down_w.shape[1]
    rps, npair = rows // ns, ns // 2
    tn = tile_of(hcols, (896, 512, 384, 256, 128))
    tw = tile_of(tn, (896, 256, 128))
    dn = tile_of(dcols, (512, 256, 128))
    dw = tile_of(dn, (256, 128))
    nc, nd = hcols // tn, dcols // dn
    lead = min(2, nc)
    cfg = dict(
        nt=nt, ns=ns, req=nreq, kept=kept, rb=rb, rank=rank2 // 2, rows=rows, hcols=hcols, dcols=dcols,
        tn=tn, tw=tw, dn=dn, dw=dw, lead=lead,
    )
    omaps = omaps.reshape(kept, rr, omaps.shape[3])
    dma = pltpu.SemaphoreType.DMA
    scratch = [
        pltpu.VMEM((rows, fcols), BF16),
        pltpu.VMEM((2, fcols, hcols), BF16),
        pltpu.VMEM((hcols, dcols), BF16),
        pltpu.VMEM(imaps.shape, BF16),
        pltpu.VMEM(omaps.shape, BF16),
        pltpu.VMEM((nt, nreq * rr, hcols), BF16),
        pltpu.VMEM((nt, nreq * rr, hcols), BF16),
        pltpu.VMEM((ns, rr, rows), F32),
        pltpu.VMEM((ns, rr, rows), F32),
        pltpu.VMEM((rr, rows), BF16),
        pltpu.VMEM((nt, rr, rows), BF16),
        pltpu.VMEM((2, rows, rr), BF16),
        pltpu.VMEM((lead, 2, rows, tn), F32),
        pltpu.VMEM((2, rows, hcols), BF16),
        pltpu.VMEM((npair, 2, rps, hcols), BF16),
        pltpu.VMEM((npair, 2, rps, hcols), BF16),
        pltpu.VMEM((npair, 2, rps, hcols), BF16),
        pltpu.VMEM((rows, hcols), BF16),
        pltpu.VMEM((rows, dcols), BF16),
        pltpu.VMEM((nt, rpt, dcols), BF16),
        dma((3,)),
        dma((2, nc)),
        dma((nd,)),
        dma((nt,)), dma((nt,)),
        dma((nt, nc)), dma((nt, nc)),
        dma((ns,)), dma((ns,)),
        dma((nt,)), dma((nt,)),
        dma((npair, nc)), dma((npair, nc)),
        dma((npair, nc)), dma((npair, nc)),
        dma((npair, nc)), dma((npair, nc)),
        dma((npair, nc)), dma((npair, nc)),
        dma((nt, nd)), dma((nt, nd)),
    ]
    any_space = pl.BlockSpec(memory_space=pl.ANY)
    smem = pl.BlockSpec(memory_space=pltpu.SMEM)
    weight_bytes = 2 * (2 * fcols * hcols + hcols * dcols)
    return pl.pallas_call(
        functools.partial(block_kernel, cfg),
        out_shape=jax.ShapeDtypeStruct((rpt, dcols), BF16),
        in_specs=[smem, smem] + [any_space] * 6,
        out_specs=pl.BlockSpec(memory_space=pltpu.VMEM),
        scratch_shapes=scratch,
        compiler_params=pltpu.CompilerParams(
            collective_id=0, has_side_effects=True, vmem_limit_bytes=60 * 1024 * 1024
        ),
        cost_estimate=pl.CostEstimate(
            flops=rows * weight_bytes, bytes_accessed=weight_bytes, transcendentals=rps * hcols
        ),
    )(ids, slots, tokens, gate_w, up_w, down_w, imaps, omaps)


def solution(mesh):
    in_specs = (
        P(("groups", "tensor"), "sub"),
        P("groups"),
        P("groups"),
        P("sub", "tensor"),
        P("sub", "tensor"),
        P("tensor", "sub"),
        P(("groups", "tensor"), "sub", None),
        P(("groups", "tensor"), None, "sub", None),
    )
    out_specs = P(("groups", "tensor"), "sub")
    return jax.shard_map(
        functools.partial(shards, mesh), mesh=mesh, in_specs=in_specs, out_specs=out_specs, check_vma=False
    )
```

```python
import functools

import jax
import jax.numpy as jnp
from jax import lax
from jax.experimental import pallas as pl
from jax.experimental.pallas import tpu as pltpu
from jax.sharding import PartitionSpec as P

MESH = pl.DeviceIdType.MESH
F32 = jnp.float32
BF16 = jnp.bfloat16


def tile_of(width, choices):
    for choice in choices:
        if width % choice == 0:
            return choice
    return width


def aligned(index, size):
    return pl.ds(pl.multiple_of(index * size, size), size)


def block_kernel(
    cfg,
    ids_ref,
    slots_ref,
    tok_hbm,
    gate_hbm,
    up_hbm,
    down_hbm,
    imap_hbm,
    omap_hbm,
    out_ref,
    x_buf,
    w_buf,
    d_buf,
    imap,
    omap,
    b_send,
    b_recv,
    sh1_send,
    sh1_recv,
    sh2_send,
    sh2_recv,
    s_cols,
    acc,
    part,
    p_recv,
    x_send,
    x_recv,
    hid,
    d_part,
    d_recv,
    load_sem,
    w_sem,
    dw_sem,
    tok_s,
    tok_r,
    b_s,
    b_r,
    sh1_s,
    sh1_r,
    sh2_s,
    sh2_r,
    p_s,
    p_r,
    x_s,
    x_r,
    h_s,
    h_r,
    f_s,
    f_r,
    d_s,
    d_r,
):
    nt, ns, nreq, kept, rb, rank = cfg["nt"], cfg["ns"], cfg["req"], cfg["kept"], cfg["rb"], cfg["rank"]
    rows, hcols, dcols = cfg["rows"], cfg["hcols"], cfg["dcols"]
    tn, tw, dn, dw = cfg["tn"], cfg["tw"], cfg["dn"], cfg["dw"]
    nc, nd, lead = hcols // tn, dcols // dn, cfg["lead"]
    rpt, rps, blk, npair = rows // nt, rows // ns, rows // nreq, ns // 2
    rr = 2 * rb
    t = lax.axis_index("tensor")
    s = lax.axis_index("sub")
    pair, core = lax.div(s, 2), lax.rem(s, 2)
    mate = pair * 2 + (1 - core)
    t_peers = [lax.rem(t + i, nt) for i in range(1, nt)]
    s_peers = [lax.rem(s + i, ns) for i in range(1, ns)]
    j_peers = [lax.rem(pair + i, npair) for i in range(1, npair)]

    def remote(src, dst, ssem, rsem, dev):
        return pltpu.make_async_remote_copy(
            src_ref=src, dst_ref=dst, send_sem=ssem, recv_sem=rsem, device_id=dev, device_id_type=MESH
        )

    sent = []

    def send(*args):
        copy = remote(*args)
        copy.start()
        sent.append(copy)

    l_omap = pltpu.make_async_copy(omap_hbm, omap, load_sem.at[0])
    l_tok = pltpu.make_async_copy(tok_hbm, x_buf.at[aligned(t, rpt), :], load_sem.at[1])
    l_imap = pltpu.make_async_copy(imap_hbm, imap, load_sem.at[2])
    l_omap.start()
    l_tok.start()
    l_imap.start()
    l_w = []
    for k in range(nc):
        cols = pl.ds(k * tn, tn)
        pair_loads = [
            pltpu.make_async_copy(src.at[:, cols], w_buf.at[g, :, cols], w_sem.at[g, k])
            for g, src in enumerate((gate_hbm, up_hbm))
        ]
        for copy in pair_loads:
            copy.start()
        l_w.append(pair_loads)

    barrier = pltpu.get_barrier_semaphore()
    for p in t_peers:
        pl.semaphore_signal(barrier, inc=1, device_id={"tensor": p}, device_id_type=MESH)
    for p in s_peers:
        pl.semaphore_signal(barrier, inc=1, device_id={"sub": p}, device_id_type=MESH)
    pl.semaphore_wait(barrier, nt + ns - 2)

    for i, p in enumerate(t_peers):
        send(tok_hbm, x_buf.at[aligned(t, rpt), :], tok_s.at[i], tok_r.at[t], {"tensor": p})

    slots = [slots_ref[ids_ref[q]] for q in range(nreq)]
    local = [lax.rem(v, kept) for v in slots]
    mine = [jnp.where(lax.div(v, kept) == t, 1.0, 0.0).astype(F32) for v in slots]

    l_omap.wait()
    for q in range(nreq):
        for c in range(nt):
            theirs = omap[local[q], :, c * hcols : (c + 1) * hcols]
            b_send[c, q * rr : (q + 1) * rr, :] = (theirs.astype(F32) * mine[q]).astype(BF16)
    map_copies = []

    def send_maps():
        k = len(map_copies)
        if k == nc:
            return
        if k > 0:
            for copy in map_copies[-1]:
                copy.wait_send()
        cols = pl.ds(k * tn, tn)
        copies = [
            remote(b_send.at[p, :, cols], b_recv.at[t, :, cols], b_s.at[i, k], b_r.at[t, k], {"tensor": p})
            for i, p in enumerate(t_peers)
        ]
        for copy in copies:
            copy.start()
        map_copies.append(copies)

    l_imap.wait()
    l_tok.wait()
    for p in t_peers:
        remote(tok_hbm, x_buf.at[aligned(p, rpt), :], tok_s.at[0], tok_r.at[p], {"tensor": p}).wait_recv()

    send_maps()

    for q in range(nreq):
        span = slice(q * blk, (q + 1) * blk)
        piece = jnp.dot(x_buf[span, :], imap[local[q]], preferred_element_type=F32) * mine[q]
        flipped = piece.T
        for d in range(ns):
            sh1_send[d, 0:rb, span] = flipped[d * rb : (d + 1) * rb]
            sh1_send[d, rb:rr, span] = flipped[rank + d * rb : rank + (d + 1) * rb]
    for i, p in enumerate(s_peers):
        send(sh1_send.at[p], sh1_recv.at[s], sh1_s.at[i], sh1_r.at[s], {"sub": p})

    l_d = []
    for n in range(nd):
        cols = pl.ds(n * dn, dn)
        copy = pltpu.make_async_copy(down_hbm.at[:, cols], d_buf.at[:, cols], dw_sem.at[n])
        copy.start()
        l_d.append(copy)

    per = tn // tw

    def matmul(k):
        for copy in l_w[k]:
            copy.wait()

        def body(j, carry):
            g, c = lax.div(j, per), lax.rem(j, per)
            if per == 1:
                into, cols = pl.ds(0, tw), pl.ds(k * tn, tw)
            else:
                into, cols = aligned(c, tw), pl.ds(pl.multiple_of(k * tn + c * tw, 128), tw)
            acc[k % lead, g, :, into] = jnp.dot(x_buf[...], w_buf[g, :, cols], preferred_element_type=F32)
            return carry

        lax.fori_loop(0, 2 * per, body, 0)

    def finish(k):
        send_maps()
        cols = pl.ds(k * tn, tn)
        for p in t_peers:
            remote(
                b_send.at[p, :, cols], b_recv.at[p, :, cols], b_s.at[0, k], b_r.at[p, k], {"tensor": p}
            ).wait_recv()
        total = b_send[t, :, cols].astype(F32)
        for p in t_peers:
            total += b_recv[p, :, cols].astype(F32)
        maps = total.astype(BF16)
        for g in range(2):
            for q in range(nreq):
                span = slice(q * blk, (q + 1) * blk)
                part[g, span, cols] = (
                    acc[k % lead, g, span, :]
                    + jnp.dot(s_cols[g, span, :], maps[q * rr : (q + 1) * rr], preferred_element_type=F32)
                ).astype(BF16)
        for j in j_peers + [pair]:
            send(
                part.at[:, aligned(2 * j + 1 - core, rps), cols],
                p_recv.at[j, :, :, cols],
                p_s.at[j, k],
                p_r.at[j, k],
                {"sub": mate},
            )

    def wait_mate(j, k):
        cols = pl.ds(k * tn, tn)
        remote(
            part.at[:, aligned(2 * j + 1 - core, rps), cols],
            p_recv.at[j, :, :, cols],
            p_s.at[j, k],
            p_r.at[j, k],
            {"sub": mate},
        ).wait_recv()

    def across(k):
        cols = pl.ds(k * tn, tn)
        for j in j_peers:
            wait_mate(j, k)
            x_send[j, :, :, cols] = (
                part[:, aligned(2 * j + core, rps), cols].astype(F32) + p_recv[j, :, :, cols].astype(F32)
            ).astype(BF16)
            send(
                x_send.at[j, :, :, cols],
                x_recv.at[pair, :, :, cols],
                x_s.at[j, k],
                x_r.at[pair, k],
                {"sub": 2 * j + core},
            )

    def activate(k):
        cols = pl.ds(k * tn, tn)
        wait_mate(pair, k)
        total = part[:, aligned(s, rps), cols].astype(F32) + p_recv[pair, :, :, cols].astype(F32)
        for j in j_peers:
            remote(
                x_send.at[j, :, :, cols],
                x_recv.at[j, :, :, cols],
                x_s.at[j, k],
                x_r.at[j, k],
                {"sub": 2 * j + core},
            ).wait_recv()
            total += x_recv[j, :, :, cols].astype(F32)
        gate, up = total[0], total[1]
        mine_rows = hid.at[aligned(s, rps), cols]
        hid[aligned(s, rps), cols] = (gate / (1.0 + jnp.exp(-gate)) * up).astype(BF16)
        for j in j_peers:
            send(mine_rows, mine_rows, h_s.at[j, k], h_r.at[pair, k], {"sub": 2 * j + core})
        send(mine_rows, mine_rows, f_s.at[pair, k], f_r.at[pair, k], {"sub": mate})

    def relay(k):
        cols = pl.ds(k * tn, tn)
        for j in j_peers:
            theirs = hid.at[aligned(2 * j + core, rps), cols]
            remote(theirs, theirs, h_s.at[j, k], h_r.at[j, k], {"sub": 2 * j + core}).wait_recv()
            send(theirs, theirs, f_s.at[j, k], f_r.at[j, k], {"sub": mate})

    matmul(0)

    mine_sum = sh1_send[s]
    for p in s_peers:
        remote(sh1_send.at[p], sh1_recv.at[p], sh1_s.at[0], sh1_r.at[p], {"sub": p}).wait_recv()
        mine_sum += sh1_recv[p]
    sh2_send[...] = mine_sum.astype(BF16)
    for i, p in enumerate(t_peers):
        send(sh2_send, sh2_recv.at[t], sh2_s.at[i], sh2_r.at[t], {"tensor": p})

    send_maps()
    for k in range(1, lead):
        matmul(k)

    shrink = sh2_send[...].astype(F32)
    for p in t_peers:
        remote(sh2_send, sh2_recv.at[p], sh2_s.at[0], sh2_r.at[p], {"tensor": p}).wait_recv()
        shrink += sh2_recv[p].astype(F32)
    is_gate = lax.broadcasted_iota(jnp.int32, (rr, rows), 0) < rb
    for g, chosen in enumerate((jnp.where(is_gate, shrink, 0.0), jnp.where(is_gate, 0.0, shrink))):
        for q in range(nreq):
            span = slice(q * blk, (q + 1) * blk)
            s_cols[g, span, :] = chosen[:, span].T.astype(BF16)

    for k in range(nc + 3):
        if k < nc:
            finish(k)
            if k + lead < nc:
                matmul(k + lead)
        if 0 <= k - 1 < nc:
            across(k - 1)
        if 0 <= k - 2 < nc:
            activate(k - 2)
        if 0 <= k - 3 < nc:
            relay(k - 3)

    for k in range(nc):
        cols = pl.ds(k * tn, tn)
        for j in j_peers + [pair]:
            theirs = hid.at[aligned(2 * j + 1 - core, rps), cols]
            remote(theirs, theirs, f_s.at[j, k], f_r.at[j, k], {"sub": mate}).wait_recv()

    for n in range(nd):
        l_d[n].wait()

        def down(c, carry, n=n):
            cols = pl.ds(pl.multiple_of(n * dn + c * dw, 128), dw)
            d_part[:, cols] = jnp.dot(hid[...], d_buf[:, cols], preferred_element_type=F32).astype(BF16)
            return carry

        lax.fori_loop(0, dn // dw, down, 0)
        cols = pl.ds(n * dn, dn)
        for i, p in enumerate(t_peers):
            send(
                d_part.at[aligned(p, rpt), cols],
                d_recv.at[t, :, cols],
                d_s.at[i, n],
                d_r.at[t, n],
                {"tensor": p},
            )

    for n in range(nd):
        cols = pl.ds(n * dn, dn)
        total = d_part[aligned(t, rpt), cols].astype(F32)
        for p in t_peers:
            remote(
                d_part.at[aligned(p, rpt), cols],
                d_recv.at[p, :, cols],
                d_s.at[0, n],
                d_r.at[p, n],
                {"tensor": p},
            ).wait_recv()
            total += d_recv[p, :, cols].astype(F32)
        out_ref[:, cols] = (x_buf[aligned(t, rpt), cols].astype(F32) + total).astype(BF16)

    for copy in map_copies[-1] + sent:
        copy.wait_send()


def shards(mesh, tokens, ids, slots, gate_w, up_w, down_w, imaps, omaps):
    nt, ns = mesh.shape["tensor"], mesh.shape["sub"]
    kept, fcols, rank2 = imaps.shape
    rb = omaps.shape[2]
    rr = 2 * rb
    nreq = ids.shape[0]
    rpt = tokens.shape[0]
    rows = rpt * nt
    hcols, dcols = gate_w.shape[1], down_w.shape[1]
    rps, npair = rows // ns, ns // 2
    tn = tile_of(hcols, (896, 512, 384, 256, 128))
    tw = tile_of(tn, (896, 256, 128))
    dn = tile_of(dcols, (512, 256, 128))
    dw = tile_of(dn, (256, 128))
    nc, nd = hcols // tn, dcols // dn
    lead = min(2, nc)
    cfg = dict(
        nt=nt, ns=ns, req=nreq, kept=kept, rb=rb, rank=rank2 // 2, rows=rows, hcols=hcols, dcols=dcols,
        tn=tn, tw=tw, dn=dn, dw=dw, lead=lead,
    )
    omaps = omaps.reshape(kept, rr, omaps.shape[3])
    dma = pltpu.SemaphoreType.DMA
    scratch = [
        pltpu.VMEM((rows, fcols), BF16),
        pltpu.VMEM((2, fcols, hcols), BF16),
        pltpu.VMEM((hcols, dcols), BF16),
        pltpu.VMEM(imaps.shape, BF16),
        pltpu.VMEM(omaps.shape, BF16),
        pltpu.VMEM((nt, nreq * rr, hcols), BF16),
        pltpu.VMEM((nt, nreq * rr, hcols), BF16),
        pltpu.VMEM((ns, rr, rows), F32),
        pltpu.VMEM((ns, rr, rows), F32),
        pltpu.VMEM((rr, rows), BF16),
        pltpu.VMEM((nt, rr, rows), BF16),
        pltpu.VMEM((2, rows, rr), BF16),
        pltpu.VMEM((lead, 2, rows, tn), F32),
        pltpu.VMEM((2, rows, hcols), BF16),
        pltpu.VMEM((npair, 2, rps, hcols), BF16),
        pltpu.VMEM((npair, 2, rps, hcols), BF16),
        pltpu.VMEM((npair, 2, rps, hcols), BF16),
        pltpu.VMEM((rows, hcols), BF16),
        pltpu.VMEM((rows, dcols), BF16),
        pltpu.VMEM((nt, rpt, dcols), BF16),
        dma((3,)),
        dma((2, nc)),
        dma((nd,)),
        dma((nt,)), dma((nt,)),
        dma((nt, nc)), dma((nt, nc)),
        dma((ns,)), dma((ns,)),
        dma((nt,)), dma((nt,)),
        dma((npair, nc)), dma((npair, nc)),
        dma((npair, nc)), dma((npair, nc)),
        dma((npair, nc)), dma((npair, nc)),
        dma((npair, nc)), dma((npair, nc)),
        dma((nt, nd)), dma((nt, nd)),
    ]
    any_space = pl.BlockSpec(memory_space=pl.ANY)
    smem = pl.BlockSpec(memory_space=pltpu.SMEM)
    weight_bytes = 2 * (2 * fcols * hcols + hcols * dcols)
    return pl.pallas_call(
        functools.partial(block_kernel, cfg),
        out_shape=jax.ShapeDtypeStruct((rpt, dcols), BF16),
        in_specs=[smem, smem] + [any_space] * 6,
        out_specs=pl.BlockSpec(memory_space=pltpu.VMEM),
        scratch_shapes=scratch,
        compiler_params=pltpu.CompilerParams(
            collective_id=0, has_side_effects=True, vmem_limit_bytes=60 * 1024 * 1024
        ),
        cost_estimate=pl.CostEstimate(
            flops=rows * weight_bytes, bytes_accessed=weight_bytes, transcendentals=rps * hcols
        ),
    )(ids, slots, tokens, gate_w, up_w, down_w, imaps, omaps)


def solution(mesh):
    in_specs = (
        P(("groups", "tensor"), "sub"),
        P("groups"),
        P("groups"),
        P("sub", "tensor"),
        P("sub", "tensor"),
        P("tensor", "sub"),
        P(("groups", "tensor"), "sub", None),
        P(("groups", "tensor"), None, "sub", None),
    )
    out_specs = P(("groups", "tensor"), "sub")
    return jax.shard_map(
        functools.partial(shards, mesh), mesh=mesh, in_specs=in_specs, out_specs=out_specs, check_vma=False
    )
```
